1024 devices in a mesh: rep: 16 (over x, z_hi, core), fsdp: 64 (over y, z_lo).
Axes of the slice: x: 4, y: 8, z: 16 (z_hi: 2, z_lo: 8; z = z_hi * 8 + z_lo), core: 2. Of those that a mesh axis runs over, the one named last changes fastest.
Arguments:
- activations: bfloat16 [16, 16384, 4096], P('rep', 'fsdp'), may hold values from -6 to 6
- key_cotangent: bfloat16 [16, 16384, 512], P('rep', 'fsdp'), may hold values from -6 to 6
- local_params: float32 [16, 8, 131072], P('rep', None, 'fsdp'), may hold values from -6 to 6
- anchor: float32 [8, 131072], P(None, 'fsdp'), may hold values from -6 to 6
- momentum: float32 [8, 131072], P(None, 'fsdp'), may hold values from -3 to 3
- layer_fragment: int32 [8], replicated, may hold values from 0 to 3, as said below
Outputs:
- key_grad: float32 [16, 4096, 512], P('rep', 'fsdp')
- new_anchor: float32 [8, 131072], P(None, 'fsdp')
- new_momentum: float32 [8, 131072], P(None, 'fsdp')
The draws below stay inside these ranges and needn't reach their ends.
Inputs may be any that keep to these rules, and one draw needn't show every extreme that they name: `layer_fragment`: every fragment is assigned exactly 2 layers.
All inputs are finite; a program needn't handle non-finite values.
Results may differ from the reference program's by a relative error of at most 0.0003.
Values may be sent and summed in bfloat16 or wider, within the bound.
No kernel may reach another device: no remote copies, remote signals or barrier semaphores. Data moves between devices by JAX's collectives and lax.ppermute only.
A program may use at most 64 MiB of HBM per device.

```python
import jax
import jax.numpy as jnp
from jax import lax

D = 4096
LAYERS = 8
FRAGS = 4
KVW = 512
TOKENS = 16384
ENT = 131072
REPLICAS = 16


def draw_layer_fragment(key, part):
    key = jax.random.fold_in(key, 7)
    order = jax.random.permutation(key, LAYERS)
    return (order % FRAGS).astype(jnp.int32)


def level_of(stream_key, shape, split, low, high):
    level, own = 1.0, jax.random.fold_in(stream_key, 6)
    for position, parts in split:
        draws = jnp.exp(jax.random.uniform(jax.random.fold_in(own, position), (parts,), jnp.float32, low / len(split), high / len(split)))
        level = level * jnp.repeat(draws, shape[position] // parts).reshape([-1 if axis == position else 1 for axis in range(len(shape))])
    return level


def normal_values(rng, extent, scale, most, shards=(), held_as=jnp.bfloat16):
    values = scale * jax.random.normal(rng, extent, jnp.float32)
    if shards:
        values = values * level_of(rng, extent, shards, -0.22, 0.18)
    return jnp.clip(values, -most, most).astype(held_as)


def setup_inputs(seed: int = 0) -> dict:
    keys = jax.random.split(jax.random.key(seed), 7)
    return {
        "activations": normal_values(keys[0], (REPLICAS, TOKENS, D), 1.0, 6.0, ((0, 16), (1, 64))),
        "key_cotangent": normal_values(keys[1], (REPLICAS, TOKENS, KVW), 1.0, 6.0, ((0, 16), (1, 64))),
        "local_params": normal_values(keys[2], (REPLICAS, LAYERS, ENT), 1.0, 6.0, ((0, 16), (2, 64)), jnp.float32),
        "anchor": normal_values(keys[3], (LAYERS, ENT), 1.0, 6.0, ((1, 64),), jnp.float32),
        "momentum": normal_values(keys[4], (LAYERS, ENT), 0.5, 3.0, ((1, 64),), jnp.float32),
        "layer_fragment": draw_layer_fragment(jax.random.fold_in(keys[6], 71), 0),
    }


outer_rate = 0.7
momentum_keep = 0.9

def group_grad(pair):
    inputs, cotangent = pair
    return lax.dot_general(inputs, cotangent, (((0,), (0,)), ((), ())), preferred_element_type=jnp.float32)

def reference(activations, key_cotangent, local_params, anchor, momentum, layer_fragment):
    groups = activations.shape[0]
    tokens = activations.shape[1]
    key_grad = lax.map(group_grad, (activations, key_cotangent)) * float(tokens) ** (-0.5)
    delta = lax.optimization_barrier(jnp.sum(anchor[None] - local_params, axis=0)) / groups
    chosen = (layer_fragment == 0)[:, None]
    moved = momentum_keep * momentum + delta
    new_momentum = jnp.where(chosen, moved, momentum)
    new_anchor = jnp.where(chosen, anchor - outer_rate * (delta + momentum_keep * moved), anchor)
    return (key_grad, new_anchor, new_momentum)
```

```python
import functools
import math

import jax
import jax.numpy as jnp
from jax import lax
from jax.experimental import pallas as pl
from jax.experimental.pallas import tpu as pltpu
from jax.sharding import PartitionSpec as P

outer_rate = 0.7
momentum_keep = 0.9
ring, line = 8, 8
group = 64
tail = 16
steps_per_octave = 8.0
top = 32760.0
whole = pl.BlockSpec(memory_space=pltpu.VMEM)
limit = pltpu.CompilerParams(vmem_limit_bytes=40 * 1024 * 1024)


def code(values, out, at=None):
    count = values.shape[0] // group
    exponents = []
    for g in range(count):
        part = values[g * group:(g + 1) * group]
        most = jnp.max(jnp.abs(part), axis=0, keepdims=True)
        exponent = jnp.ceil(jnp.log(jnp.maximum(most, 1e-30)) * (steps_per_octave / math.log(2.0))) + 1.0
        inverse = jnp.exp(exponent * (-math.log(2.0) / steps_per_octave)) * top
        magic = 12582912.0
        coded = (part * inverse + magic) - magic
        out[g * group:(g + 1) * group, :] = coded.astype(jnp.int32).astype(jnp.int16)
        exponents.append(exponent)
    exponents.append(jnp.zeros((tail - count, values.shape[1]), jnp.float32))
    out[count * group:count * group + tail, :] = jnp.concatenate(exponents, axis=0).astype(jnp.int32).astype(jnp.int16)


def scales(message):
    rows = message.shape[0] - tail
    exponents = message[rows:rows + tail, :].astype(jnp.int32).astype(jnp.float32)
    return jnp.exp(exponents * (math.log(2.0) / steps_per_octave)) * (1.0 / top)


def decoded(message, scale, g):
    return message[g * group:(g + 1) * group, :].astype(jnp.int32).astype(jnp.float32) * scale[g:g + 1]


def product(left, right):
    return lax.dot_general(left, right, (((0,), (0,)), ((), ())), preferred_element_type=jnp.float32)


def sums_kernel(place, own_here, own_up, own_down, cotangent, from_below, from_above, up, down, here):
    width = own_here.shape[1]
    half = width // 2
    mine = cotangent[...]
    keys = from_below.shape[1] - mine.shape[1]
    below = from_below[:, keys:]
    above = from_above[:, keys:]
    here[...] = (
        product(own_here[...], mine)
        + product(from_below[:, :width], below)
        + product(from_above[:, :width], above)
    )
    rest = product(own_up[...], mine) + product(from_above[:, width:2 * width], above)
    first = product(from_below[:, 2 * width:keys], below)
    code(jnp.concatenate([rest[:half] + first, rest[half:]], axis=0), up)
    rest = product(own_down[...], mine) + product(from_below[:, width:2 * width], below)
    last = product(from_above[:, 2 * width:keys], above)
    code(jnp.concatenate([rest[:half], rest[half:] + last], axis=0), down)


def sums(place, activations, cotangent, from_below, from_above):
    tokens, width = cotangent.shape[0], activations.shape[1] // ring
    columns = cotangent.shape[1]

    def block(shift):
        return pl.BlockSpec((tokens, width), lambda i, place: (0, lax.rem(place[0] + shift + ring, ring)))

    full = lambda a: pl.BlockSpec(a.shape, lambda i, place: (0, 0))
    outs = [
        jax.ShapeDtypeStruct((width + tail, columns), jnp.int16),
        jax.ShapeDtypeStruct((width + tail, columns), jnp.int16),
        jax.ShapeDtypeStruct((width, columns), jnp.float32),
    ]
    return pl.pallas_call(
        sums_kernel,
        out_shape=outs,
        grid_spec=pltpu.PrefetchScalarGridSpec(
            num_scalar_prefetch=1,
            grid=(1,),
            in_specs=[block(0), block(3), block(-3), full(cotangent), full(from_below), full(from_above)],
            out_specs=[full(o) for o in outs],
        ),
        compiler_params=limit,
    )(place, activations, activations, activations, cotangent, from_below, from_above)


def fold_kernel(arrived, bit, *refs):
    place, kept = refs[0], refs[1]
    messages = refs[2:2 + arrived]
    sent, out, total = refs[2 + arrived:]
    factors = [scales(m) for m in messages]
    count = kept.shape[0] // group
    side = place[0]
    for g in range(count):
        value = kept[g * group:(g + 1) * group, :]
        for m, f in zip(messages, factors):
            value = value + decoded(m, f, g)
        total[g % 2, (g // 2) * group:(g // 2 + 1) * group, :] = value
    out[...] = total[side]
    code(total[1 - side], sent)


def fold(side, kept, messages):
    rows, columns = kept.shape
    outs = [
        jax.ShapeDtypeStruct((rows // 2 + tail, columns), jnp.int16),
        jax.ShapeDtypeStruct((rows // 2, columns), jnp.float32),
    ]
    return pl.pallas_call(
        functools.partial(fold_kernel, len(messages), None),
        out_shape=outs,
        in_specs=[pl.BlockSpec(memory_space=pltpu.SMEM)] + [whole] * (1 + len(messages)),
        out_specs=[whole, whole],
        scratch_shapes=[pltpu.VMEM((2, rows // 2, columns), jnp.float32)],
        compiler_params=limit,
    )(side, kept, *messages)


def last_kernel(scale, kept, message, out):
    out[...] = (kept[...] + decoded(message, scales(message), 0)) * scale


def last(scale, kept, message):
    return pl.pallas_call(
        functools.partial(last_kernel, scale),
        out_shape=jax.ShapeDtypeStruct(kept.shape, jnp.float32),
        in_specs=[whole, whole],
        out_specs=whole,
        compiler_params=limit,
    )(kept, message)


def along_ring(shift):
    return [(y * line + z, ((y + shift) % ring) * line + z) for y in range(ring) for z in range(line)]


def along_line(bit):
    return [(y * line + z, y * line + (z ^ bit)) for y in range(ring) for z in range(line)]


def gradient(inputs, cotangent):
    tokens, features = inputs.shape
    width = features // ring
    at = lax.axis_index("fsdp")
    y, z = at // line, at % line

    def chunk(shift, start=0, size=width):
        return lax.dynamic_slice_in_dim(inputs, lax.rem(y + shift + ring, ring) * width + start, size, 1)

    half = width // 2
    with jax.named_scope("inputs_to_neighbours"):
        above = jnp.concatenate([chunk(1), chunk(-2), chunk(4, 0, half), cotangent], axis=1)
        below = jnp.concatenate([chunk(-1), chunk(2), chunk(4, half, half), cotangent], axis=1)
        from_below = lax.ppermute(above, "fsdp", along_ring(1))
        from_above = lax.ppermute(below, "fsdp", along_ring(-1))
    place = jnp.full((1,), y, jnp.int32)
    up, down, here = sums(place, inputs, cotangent, from_below, from_above)
    with jax.named_scope("sums_along_ring"):
        messages = [lax.ppermute(up, "fsdp", along_ring(3)), lax.ppermute(down, "fsdp", along_ring(-3))]
    kept = here
    bit = 1
    while bit < line:
        side = jnp.full((1,), (z // bit) % 2, jnp.int32)
        sent, kept = fold(side, kept, messages)
        with jax.named_scope("sums_along_line"):
            messages = [lax.ppermute(sent, "fsdp", along_line(bit))]
        bit *= 2
    return last(float(tokens * ring * line) ** (-0.5), kept, messages[0])


def outer_step(local, anchor, momentum, layer_fragment):
    groups = lax.axis_size("rep")
    chosen = layer_fragment == 0
    order = jnp.cumsum(chosen.astype(jnp.int32))
    picks = [(chosen & (order == i + 1))[:, None] for i in range(2)]
    delta = anchor - local
    total = jnp.stack([jnp.sum(jnp.where(p, delta, 0.0), axis=0) for p in picks])
    with jax.named_scope("differences_over_replicas"):
        bit = 1
        while bit < groups:
            total = total + lax.ppermute(total, "rep", [(r, r ^ bit) for r in range(groups)])
            bit *= 2
    average = total / groups
    average = jnp.where(picks[0], average[0:1], average[1:2])
    moved = momentum_keep * momentum + average
    mask = chosen[:, None]
    new_anchor = jnp.where(mask, anchor - outer_rate * (average + momentum_keep * moved), anchor)
    return new_anchor, jnp.where(mask, moved, momentum)


def body(activations, key_cotangent, local_params, anchor, momentum, layer_fragment):
    key_grad = gradient(activations[0], key_cotangent[0])[None]
    new_anchor, new_momentum = outer_step(local_params[0], anchor, momentum, layer_fragment)
    return (key_grad, new_anchor, new_momentum)


def solution(mesh):
    placed = (
        P("rep", "fsdp", None),
        P("rep", "fsdp", None),
        P("rep", None, "fsdp"),
        P(None, "fsdp"),
        P(None, "fsdp"),
        P(),
    )
    return jax.shard_map(
        body,
        mesh=mesh,
        in_specs=placed,
        out_specs=(P("rep", "fsdp", None), P(None, "fsdp"), P(None, "fsdp")),
        check_vma=False,
    )
```

```python
import functools
import math

import jax
import jax.numpy as jnp
from jax import lax
from jax.experimental import pallas as pl
from jax.experimental.pallas import tpu as pltpu
from jax.sharding import PartitionSpec as P

outer_rate = 0.7
momentum_keep = 0.9
ring, line = 8, 8
group = 64
tail = 16
steps_per_octave = 8.0
top = 32760.0
whole = pl.BlockSpec(memory_space=pltpu.VMEM)
anywhere = pl.BlockSpec(memory_space=pl.ANY)
limit = pltpu.CompilerParams(vmem_limit_bytes=40 * 1024 * 1024)


def work(micros):
    return pl.CostEstimate(flops=0, bytes_accessed=micros * 3000000, transcendentals=0)


def code(values, out):
    count = values.shape[0] // group
    exponents = []
    for g in range(count):
        part = values[g * group:(g + 1) * group, :]
        most = jnp.max(jnp.abs(part), axis=0, keepdims=True)
        exponent = jnp.ceil(jnp.log(jnp.maximum(most, 1e-30)) * (steps_per_octave / math.log(2.0))) + 1.0
        inverse = jnp.exp(exponent * (-math.log(2.0) / steps_per_octave)) * top
        magic = 12582912.0
        coded = (part * inverse + magic) - magic
        out[g * group:(g + 1) * group, :] = coded.astype(jnp.int32).astype(jnp.int16)
        exponents.append(exponent)
    exponents.append(jnp.zeros((tail - count, values.shape[1]), jnp.float32))
    out[count * group:count * group + tail, :] = jnp.concatenate(exponents, axis=0).astype(jnp.int32).astype(jnp.int16)


def scales(message):
    rows = message.shape[0] - tail
    exponents = message[rows:rows + tail, :].astype(jnp.int32).astype(jnp.float32)
    return jnp.exp(exponents * (math.log(2.0) / steps_per_octave)) * (1.0 / top)


def decoded(message, scale, g):
    return message[g * group:(g + 1) * group, :].astype(jnp.int32).astype(jnp.float32) * scale[g:g + 1]


def product(left, right):
    return lax.dot_general(left, right, (((0,), (0,)), ((), ())), preferred_element_type=jnp.float32)


def chunk_of(activations, shift):
    width = activations.shape[1] // ring
    return pl.BlockSpec((activations.shape[0], width), lambda i, place: (0, lax.rem(place[0] + shift + ring, ring)))


def on_chunks(kernel, place, inputs, outs, scratch=(), mebibytes=40):
    full = lambda a: pl.BlockSpec(a.shape, lambda i, place: (0, 0))
    specs = [chunk_of(*a) if isinstance(a, tuple) else full(a) for a in inputs]
    return pl.pallas_call(
        kernel,
        out_shape=outs,
        grid_spec=pltpu.PrefetchScalarGridSpec(
            num_scalar_prefetch=1,
            grid=(1,),
            in_specs=specs,
            out_specs=[full(o) for o in outs],
            scratch_shapes=[pltpu.VMEM(shape, jnp.float32) for shape in scratch],
        ),
        compiler_params=pltpu.CompilerParams(vmem_limit_bytes=mebibytes * 1024 * 1024),
        cost_estimate=work(1),
    )(place, *[a[0] if isinstance(a, tuple) else a for a in inputs])


def pack_kernel(place, next_up, next_down, up, down, across, cotangent, above, below):
    width = up.shape[1]
    half = width // 2
    above[:, :width] = next_up[...]
    below[:, :width] = next_down[...]
    above[:, width:2 * width] = down[...]
    below[:, width:2 * width] = up[...]
    above[:, 2 * width:2 * width + half] = across[:, :half]
    below[:, 2 * width:2 * width + half] = across[:, half:]
    above[:, 2 * width + half:] = cotangent[...]
    below[:, 2 * width + half:] = cotangent[...]


def pack(place, activations, cotangent):
    columns = activations.shape[1] // ring * 5 // 2 + cotangent.shape[1]
    out = jax.ShapeDtypeStruct((activations.shape[0], columns), activations.dtype)
    inputs = [(activations, shift) for shift in (1, -1, 2, -2, 4)] + [cotangent]
    return on_chunks(pack_kernel, place, inputs, [out, out], mebibytes=60)


def part(source, total, side, kept, sent):
    for g in range(source.shape[0] // group):
        total[g % 2, g // 2 * group:(g // 2 + 1) * group, :] = source[g * group:(g + 1) * group, :]
    kept[...] = total[side]
    code(total.at[1 - side], sent)


def sums_kernel(place, own, own_up, own_down, cotangent, below, above, far_sent, far_kept, near_sent, near_kept,
                far, near, far_parted, near_parted):
    width = own.shape[1]
    half = width // 2
    keys = 2 * width + half
    mine, under, over = cotangent[...], below[:, keys:], above[:, keys:]
    far[:width] = product(own_up[...], mine) + product(above[:, width:2 * width], over)
    far[:half] += product(below[:, 2 * width:keys], under)
    far[width:] = product(own_down[...], mine) + product(below[:, width:2 * width], under)
    far[width + half:] += product(above[:, 2 * width:keys], over)
    part(far, far_parted, place[1], far_kept, far_sent)
    near[...] = product(own[...], mine) + product(below[:, :width], under) + product(above[:, :width], over)
    part(near, near_parted, place[1], near_kept, near_sent)


def sums(place, activations, cotangent, from_below, from_above):
    width = activations.shape[1] // ring
    half = width // 2
    columns = cotangent.shape[1]
    outs = [
        jax.ShapeDtypeStruct((width + tail, columns), jnp.int16),
        jax.ShapeDtypeStruct((width, columns), jnp.float32),
        jax.ShapeDtypeStruct((half + tail, columns), jnp.int16),
        jax.ShapeDtypeStruct((half, columns), jnp.float32),
    ]
    inputs = [(activations, 0), (activations, 3), (activations, -3), cotangent, from_below, from_above]
    scratch = [(2 * width, columns), (width, columns), (2, width, columns), (2, half, columns)]
    return on_chunks(sums_kernel, place, inputs, outs, scratch)


def call(kernel, outs, place, *args, scratch=(), micros=1):
    return pl.pallas_call(
        kernel,
        out_shape=[jax.ShapeDtypeStruct(s, d) for s, d in outs],
        in_specs=[pl.BlockSpec(memory_space=pltpu.SMEM)] + [whole] * len(args),
        out_specs=[whole] * len(outs),
        scratch_shapes=[pltpu.VMEM(s, jnp.float32) for s in scratch],
        compiler_params=limit,
        cost_estimate=work(micros),
    )(place, *args)


def rest_kernel(place, kept, message, up, down, sums):
    scale = scales(message)
    for g in range(kept.shape[0] // group):
        sums[g * group:(g + 1) * group, :] = kept[g * group:(g + 1) * group, :] + decoded(message, scale, g)
    rows = kept.shape[0] // 2
    code(sums.at[:rows], up)
    code(sums.at[rows:], down)


def rest(place, kept, message):
    rows, columns = kept.shape
    coded = ((rows // 2 + tail, columns), jnp.int16)
    return call(rest_kernel, [coded, coded], place, kept, message, scratch=[(rows, columns)], micros=5)


def fold_kernel(bit, place, kept, *refs):
    messages, (sent, out, total) = refs[:-3], refs[-3:]
    factors = [scales(m) for m in messages]
    for g in range(kept.shape[0] // group):
        value = kept[g * group:(g + 1) * group, :]
        for m, factor in zip(messages, factors):
            value = value + decoded(m, factor, g)
        total[g % 2, g // 2 * group:(g // 2 + 1) * group, :] = value
    side = place[bit]
    out[...] = total[side]
    code(total.at[1 - side], sent)


def fold(place, bit, kept, messages, micros=1):
    half, columns = kept.shape[0] // 2, kept.shape[1]
    outs = [((half + tail, columns), jnp.int16), ((half, columns), jnp.float32)]
    return call(functools.partial(fold_kernel, bit), outs, place, kept, *messages, scratch=[(2, half, columns)], micros=micros)


def last_kernel(scale, place, kept, message, out):
    out[...] = (kept[...] + decoded(message, scales(message), 0)) * scale


def last(scale, place, kept, message):
    return call(functools.partial(last_kernel, scale), [(kept.shape, jnp.float32)], place, kept, message)[0]


def along_ring(shift):
    return [(y * line + z, ((y + shift) % ring) * line + z) for y in range(ring) for z in range(line)]


def along_line(bit):
    return [(y * line + z, y * line + (z ^ bit)) for y in range(ring) for z in range(line)]


def after(value, *others):
    return lax.optimization_barrier((value, *others))[0]


def outer_sums(local, anchor, layer_fragment):
    chosen = layer_fragment == 0
    order = jnp.cumsum(chosen.astype(jnp.int32))
    picks = [(chosen & (order == i + 1))[:, None] for i in range(2)]
    delta = anchor - local
    total = jnp.stack([jnp.sum(jnp.where(p, delta, 0.0), axis=0) for p in picks])
    groups = lax.axis_size("rep")

    def add_over(total, bit):
        with jax.named_scope("differences_over_replicas"):
            return total + lax.ppermute(total, "rep", [(r, r ^ bit) for r in range(groups)])

    return picks, total, add_over


def outer_step(picks, total, anchor, momentum):
    average = total / lax.axis_size("rep")
    average = jnp.where(picks[0], average[0:1], average[1:2])
    moved = momentum_keep * momentum + average
    mask = picks[0] | picks[1]
    new_anchor = jnp.where(mask, anchor - outer_rate * (average + momentum_keep * moved), anchor)
    return new_anchor, jnp.where(mask, moved, momentum)


def step(inputs, cotangent, local, anchor, momentum, layer_fragment):
    tokens, features = inputs.shape
    at = lax.axis_index("fsdp")
    y, z = lax.div(at, line), lax.rem(at, line)
    place = jnp.stack([y, lax.rem(z, 2), lax.rem(lax.div(z, 2), 2), lax.div(z, 4)]).astype(jnp.int32)

    def ring_move(a, shift):
        return lax.ppermute(a, "fsdp", along_ring(shift))

    def line_move(a, bit):
        return lax.ppermute(a, "fsdp", along_line(bit))

    with jax.named_scope("inputs_to_neighbours"):
        above, below = pack(place, inputs, cotangent)
        received = [ring_move(above, 1), ring_move(below, -1)]
    picks, total, add_over = outer_sums(local, anchor, layer_fragment)
    total = add_over(add_over(after(total, above), 2), 4)
    sent, kept, near, here = sums(after(place, total), inputs, cotangent, *received)
    with jax.named_scope("along_line_first"):
        arrived = line_move(sent, 1)
        messages = [line_move(near, 1)]
    total = add_over(add_over(after(total, sent), 1), 8)
    up, down = rest(after(place, total), kept, arrived)
    with jax.named_scope("far_along_ring"):
        messages += [ring_move(up, 3), ring_move(down, -3)]
    with jax.named_scope("along_line"):
        sent, here = fold(place, 2, here, messages)
        sent = line_move(sent, 2)
        sent, here = fold(place, 3, here, [sent])
        sent = line_move(sent, 4)
    grad = last(float(tokens * ring * line) ** (-0.5), place, here, sent)
    return (grad, *outer_step(picks, total, anchor, momentum))


def body(activations, key_cotangent, local_params, anchor, momentum, layer_fragment):
    grad, new_anchor, new_momentum = step(
        activations[0], key_cotangent[0], local_params[0], anchor, momentum, layer_fragment
    )
    return (grad[None], new_anchor, new_momentum)


def solution(mesh):
    placed = (
        P("rep", "fsdp", None),
        P("rep", "fsdp", None),
        P("rep", None, "fsdp"),
        P(None, "fsdp"),
        P(None, "fsdp"),
        P(),
    )
    return jax.shard_map(
        body,
        mesh=mesh,
        in_specs=placed,
        out_specs=(P("rep", "fsdp", None), P(None, "fsdp"), P(None, "fsdp")),
        check_vma=False,
    )
```

```python
import functools
import math

import jax
import jax.numpy as jnp
from jax import lax
from jax.experimental import pallas as pl
from jax.experimental.pallas import tpu as pltpu
from jax.sharding import PartitionSpec as P

outer_rate = 0.7
momentum_keep = 0.9
ring, line = 8, 8
group = 64
shared = 128
tail = 16
steps_per_octave = 8.0
top = 32760.0
whole = pl.BlockSpec(memory_space=pltpu.VMEM)
anywhere = pl.BlockSpec(memory_space=pl.ANY)
limit = pltpu.CompilerParams(vmem_limit_bytes=40 * 1024 * 1024)


def work(micros):
    return pl.CostEstimate(flops=0, bytes_accessed=micros * 3000000, transcendentals=0)


def code(values, out):
    count = values.shape[0] // group
    exponents = []
    for g in range(count):
        part = values[g * group:(g + 1) * group, :]
        most = jnp.max(jnp.abs(part), axis=0, keepdims=True)
        exponent = jnp.ceil(jnp.log(jnp.maximum(most, 1e-30)) * (steps_per_octave / math.log(2.0))) + 1.0
        inverse = jnp.exp(exponent * (-math.log(2.0) / steps_per_octave)) * top
        magic = 12582912.0
        coded = (part * inverse + magic) - magic
        out[g * group:(g + 1) * group, :] = coded.astype(jnp.int32).astype(jnp.int16)
        exponents.append(exponent)
    exponents.append(jnp.zeros((tail - count, values.shape[1]), jnp.float32))
    out[count * group:count * group + tail, :] = jnp.concatenate(exponents, axis=0).astype(jnp.int32).astype(jnp.int16)


def scales(message):
    rows = message.shape[0] - tail
    exponents = message[rows:rows + tail, :].astype(jnp.int32).astype(jnp.float32)
    return jnp.exp(exponents * (math.log(2.0) / steps_per_octave)) * (1.0 / top)


def decoded(message, scale, g):
    return message[g * group:(g + 1) * group, :].astype(jnp.int32).astype(jnp.float32) * scale[g:g + 1]


def product(left, right):
    return lax.dot_general(left, right, (((0,), (0,)), ((), ())), preferred_element_type=jnp.float32)


def chunk_of(activations, shift):
    width = activations.shape[1] // ring
    return pl.BlockSpec((activations.shape[0], width), lambda i, place: (0, lax.rem(place[0] + shift + ring, ring)))


def on_chunks(kernel, place, inputs, outs, scratch=(), mebibytes=40):
    full = lambda a: pl.BlockSpec(a.shape, lambda i, place: (0, 0))
    specs = [chunk_of(*a) if isinstance(a, tuple) else full(a) for a in inputs]
    return pl.pallas_call(
        kernel,
        out_shape=outs,
        grid_spec=pltpu.PrefetchScalarGridSpec(
            num_scalar_prefetch=1,
            grid=(1,),
            in_specs=specs,
            out_specs=[full(o) for o in outs],
            scratch_shapes=[pltpu.VMEM(shape, jnp.float32) for shape in scratch],
        ),
        compiler_params=pltpu.CompilerParams(vmem_limit_bytes=mebibytes * 1024 * 1024),
        cost_estimate=work(1),
    )(place, *[a[0] if isinstance(a, tuple) else a for a in inputs])


def pack_kernel(place, next_up, next_down, up, down, across, cotangent, above, below):
    width = up.shape[1]
    for message, near, far, rest in (
        (above, next_up, down, across[:, :shared]),
        (below, next_down, up, across[:, shared:]),
    ):
        keys = 2 * width + rest.shape[1]
        message[:, :width] = near[...]
        message[:, width:2 * width] = far[...]
        message[:, 2 * width:keys] = rest
        message[:, keys:] = cotangent[...]


def pack(place, activations, cotangent):
    tokens, width = activations.shape[0], activations.shape[1] // ring
    columns = 2 * width + cotangent.shape[1]
    outs = [
        jax.ShapeDtypeStruct((tokens, columns + shared), activations.dtype),
        jax.ShapeDtypeStruct((tokens, columns + width - shared), activations.dtype),
    ]
    inputs = [(activations, shift) for shift in (1, -1, 2, -2, 4)] + [cotangent]
    return on_chunks(pack_kernel, place, inputs, outs)


def part(source, total, side, kept, sent):
    for g in range(source.shape[0] // group):
        total[g % 2, g // 2 * group:(g // 2 + 1) * group, :] = source[g * group:(g + 1) * group, :]
    kept[...] = total[side]
    code(total.at[1 - side], sent)


def sums_kernel(place, own, own_up, own_down, cotangent, below, above, far_sent, far_kept, near_sent, near_kept,
                far, near, far_parted, near_parted):
    width = own.shape[1]
    mine, under, over = cotangent[...], below[:, 2 * width + shared:], above[:, 3 * width - shared:]
    far[:width] = product(own_up[...], mine) + product(above[:, width:2 * width], over)
    far[:shared] += product(below[:, 2 * width:2 * width + shared], under)
    far[width:] = product(own_down[...], mine) + product(below[:, width:2 * width], under)
    far[width + shared:] += product(above[:, 2 * width:3 * width - shared], over)
    part(far, far_parted, place[1], far_kept, far_sent)
    near[...] = product(own[...], mine) + product(below[:, :width], under) + product(above[:, :width], over)
    part(near, near_parted, place[1], near_kept, near_sent)


def sums(place, activations, cotangent, from_below, from_above):
    width = activations.shape[1] // ring
    half = width // 2
    columns = cotangent.shape[1]
    outs = [
        jax.ShapeDtypeStruct((width + tail, columns), jnp.int16),
        jax.ShapeDtypeStruct((width, columns), jnp.float32),
        jax.ShapeDtypeStruct((half + tail, columns), jnp.int16),
        jax.ShapeDtypeStruct((half, columns), jnp.float32),
    ]
    inputs = [(activations, 0), (activations, 3), (activations, -3), cotangent, from_below, from_above]
    scratch = [(2 * width, columns), (width, columns), (2, width, columns), (2, half, columns)]
    return on_chunks(sums_kernel, place, inputs, outs, scratch)


def call(kernel, outs, place, *args, scratch=(), micros=1):
    return pl.pallas_call(
        kernel,
        out_shape=[jax.ShapeDtypeStruct(s, d) for s, d in outs],
        in_specs=[pl.BlockSpec(memory_space=pltpu.SMEM)] + [whole] * len(args),
        out_specs=[whole] * len(outs),
        scratch_shapes=[pltpu.VMEM(s, jnp.float32) for s in scratch],
        compiler_params=limit,
        cost_estimate=work(micros),
    )(place, *args)


def rest_kernel(place, kept, message, up, down, sums):
    scale = scales(message)
    for g in range(kept.shape[0] // group):
        sums[g * group:(g + 1) * group, :] = kept[g * group:(g + 1) * group, :] + decoded(message, scale, g)
    rows = kept.shape[0] // 2
    code(sums.at[:rows], up)
    code(sums.at[rows:], down)


def rest(place, kept, message):
    rows, columns = kept.shape
    coded = ((rows // 2 + tail, columns), jnp.int16)
    return call(rest_kernel, [coded, coded], place, kept, message, scratch=[(rows, columns)], micros=5)


def fold_kernel(bit, place, kept, *refs):
    messages, (sent, out, total) = refs[:-3], refs[-3:]
    factors = [scales(m) for m in messages]
    for g in range(kept.shape[0] // group):
        value = kept[g * group:(g + 1) * group, :]
        for m, factor in zip(messages, factors):
            value = value + decoded(m, factor, g)
        total[g % 2, g // 2 * group:(g // 2 + 1) * group, :] = value
    side = place[bit]
    out[...] = total[side]
    code(total.at[1 - side], sent)


def fold(place, bit, kept, messages, micros=1):
    half, columns = kept.shape[0] // 2, kept.shape[1]
    outs = [((half + tail, columns), jnp.int16), ((half, columns), jnp.float32)]
    return call(functools.partial(fold_kernel, bit), outs, place, kept, *messages, scratch=[(2, half, columns)], micros=micros)


def last_kernel(scale, place, kept, message, out):
    out[...] = (kept[...] + decoded(message, scales(message), 0)) * scale


def last(scale, place, kept, message):
    return call(functools.partial(last_kernel, scale), [(kept.shape, jnp.float32)], place, kept, message)[0]


def along_ring(shift):
    return [(y * line + z, ((y + shift) % ring) * line + z) for y in range(ring) for z in range(line)]


def along_line(bit):
    return [(y * line + z, y * line + (z ^ bit)) for y in range(ring) for z in range(line)]


def after(value, *others):
    return lax.optimization_barrier((value, *others))[0]


def outer_sums(local, anchor, layer_fragment):
    chosen = layer_fragment == 0
    order = jnp.cumsum(chosen.astype(jnp.int32))
    picks = [(chosen & (order == i + 1))[:, None] for i in range(2)]
    delta = anchor - local
    total = jnp.stack([jnp.sum(jnp.where(p, delta, 0.0), axis=0) for p in picks])
    groups = lax.axis_size("rep")

    def add_over(total, bit):
        with jax.named_scope("differences_over_replicas"):
            return total + lax.ppermute(total, "rep", [(r, r ^ bit) for r in range(groups)])

    return picks, total, add_over


def outer_step(picks, total, anchor, momentum):
    average = total / lax.axis_size("rep")
    average = jnp.where(picks[0], average[0:1], average[1:2])
    moved = momentum_keep * momentum + average
    mask = picks[0] | picks[1]
    new_anchor = jnp.where(mask, anchor - outer_rate * (average + momentum_keep * moved), anchor)
    return new_anchor, jnp.where(mask, moved, momentum)


def step(inputs, cotangent, local, anchor, momentum, layer_fragment):
    tokens, features = inputs.shape
    at = lax.axis_index("fsdp")
    y, z = lax.div(at, line), lax.rem(at, line)
    place = jnp.stack([y, lax.rem(z, 2), lax.rem(lax.div(z, 2), 2), lax.div(z, 4)]).astype(jnp.int32)

    def ring_move(a, shift):
        return lax.ppermute(a, "fsdp", along_ring(shift))

    def line_move(a, bit):
        return lax.ppermute(a, "fsdp", along_line(bit))

    with jax.named_scope("inputs_to_neighbours"):
        above, below = pack(place, inputs, cotangent)
        received = [ring_move(above, 1), ring_move(below, -1)]
    picks, total, add_over = outer_sums(local, anchor, layer_fragment)
    total = add_over(add_over(after(total, above), 2), 8)
    sent, kept, near, here = sums(after(place, total), inputs, cotangent, *received)
    with jax.named_scope("along_line_first"):
        arrived = line_move(sent, 1)
        messages = [line_move(near, 1)]
    total = add_over(add_over(after(total, sent), 1), 4)
    up, down = rest(after(place, total), kept, arrived)
    with jax.named_scope("far_along_ring"):
        messages += [ring_move(up, 3), ring_move(down, -3)]
    with jax.named_scope("along_line"):
        sent, here = fold(place, 2, here, messages)
        sent = line_move(sent, 2)
        sent, here = fold(place, 3, here, [sent])
        sent = line_move(sent, 4)
    grad = last(float(tokens * ring * line) ** (-0.5), place, here, sent)
    return (grad, *outer_step(picks, total, anchor, momentum))


def body(activations, key_cotangent, local_params, anchor, momentum, layer_fragment):
    grad, new_anchor, new_momentum = step(
        activations[0], key_cotangent[0], local_params[0], anchor, momentum, layer_fragment
    )
    return (grad[None], new_anchor, new_momentum)


def solution(mesh):
    placed = (
        P("rep", "fsdp", None),
        P("rep", "fsdp", None),
        P("rep", None, "fsdp"),
        P(None, "fsdp"),
        P(None, "fsdp"),
        P(),
    )
    return jax.shard_map(
        body,
        mesh=mesh,
        in_specs=placed,
        out_specs=(P("rep", "fsdp", None), P(None, "fsdp"), P(None, "fsdp")),
        check_vma=False,
    )
```

```python
import functools
import math

import jax
import jax.numpy as jnp
from jax import lax
from jax.experimental import pallas as pl
from jax.experimental.pallas import tpu as pltpu
from jax.sharding import PartitionSpec as P

outer_rate = 0.7
momentum_keep = 0.9
ring, line = 8, 8
group = 64
shared = 128
tail = 16
steps_per_octave = 8.0
top = 32760.0
whole = pl.BlockSpec(memory_space=pltpu.VMEM)
anywhere = pl.BlockSpec(memory_space=pl.ANY)
limit = pltpu.CompilerParams(vmem_limit_bytes=40 * 1024 * 1024)


def work(micros):
    return pl.CostEstimate(flops=0, bytes_accessed=micros * 3000000, transcendentals=0)


def code(values, out):
    count = values.shape[0] // group
    exponents = []
    for g in range(count):
        part = values[g * group:(g + 1) * group, :]
        most = jnp.max(jnp.abs(part), axis=0, keepdims=True)
        exponent = jnp.ceil(jnp.log(jnp.maximum(most, 1e-30)) * (steps_per_octave / math.log(2.0))) + 1.0
        inverse = jnp.exp(exponent * (-math.log(2.0) / steps_per_octave)) * top
        magic = 12582912.0
        coded = (part * inverse + magic) - magic
        out[g * group:(g + 1) * group, :] = coded.astype(jnp.int32).astype(jnp.int16)
        exponents.append(exponent)
    exponents.append(jnp.zeros((tail - count, values.shape[1]), jnp.float32))
    out[count * group:count * group + tail, :] = jnp.concatenate(exponents, axis=0).astype(jnp.int32).astype(jnp.int16)


def scales(message):
    rows = message.shape[0] - tail
    exponents = message[rows:rows + tail, :].astype(jnp.int32).astype(jnp.float32)
    return jnp.exp(exponents * (math.log(2.0) / steps_per_octave)) * (1.0 / top)


def decoded(message, scale, g):
    return message[g * group:(g + 1) * group, :].astype(jnp.int32).astype(jnp.float32) * scale[g:g + 1]


def product(left, right):
    return lax.dot_general(left, right, (((0,), (0,)), ((), ())), preferred_element_type=jnp.float32)


def chunk_of(activations, shift):
    width = activations.shape[1] // ring
    return pl.BlockSpec((activations.shape[0], width), lambda i, place: (0, lax.rem(place[0] + shift + ring, ring)))


def on_chunks(kernel, place, inputs, outs, scratch=(), mebibytes=40):
    full = lambda a: pl.BlockSpec(a.shape, lambda i, place: (0, 0))
    specs = [chunk_of(*a) if isinstance(a, tuple) else full(a) for a in inputs]
    return pl.pallas_call(
        kernel,
        out_shape=outs,
        grid_spec=pltpu.PrefetchScalarGridSpec(
            num_scalar_prefetch=1,
            grid=(1,),
            in_specs=specs,
            out_specs=[full(o) for o in outs],
            scratch_shapes=[pltpu.VMEM(shape, jnp.float32) for shape in scratch],
        ),
        compiler_params=pltpu.CompilerParams(vmem_limit_bytes=mebibytes * 1024 * 1024),
        cost_estimate=work(1),
    )(place, *[a[0] if isinstance(a, tuple) else a for a in inputs])


def pack_kernel(activations, cotangent, above, below, sems):
    width = activations.shape[1] // ring
    y = lax.div(lax.axis_index("fsdp"), line)

    def chunk(shift, start=0, size=width):
        at = lax.rem(y + shift + ring, ring) * width + start
        return activations.at[:, pl.ds(pl.multiple_of(at, 128), size)]

    rest = width - shared
    pieces = [
        (chunk(-1), below, 0),
        (chunk(1), above, 0),
        (chunk(2), below, width),
        (chunk(-2), above, width),
        (chunk(4, shared, rest), below, 2 * width),
        (chunk(4, 0, shared), above, 2 * width),
        (cotangent, below, 2 * width + rest),
        (cotangent, above, 2 * width + shared),
    ]
    copies = [
        pltpu.make_async_copy(piece, message.at[:, pl.ds(start, piece.shape[1])], sems.at[i])
        for i, (piece, message, start) in enumerate(pieces)
    ]
    for c in copies:
        c.start()
    for c in copies:
        c.wait()


def pack(activations, cotangent):
    tokens, width = activations.shape[0], activations.shape[1] // ring
    columns = 2 * width + cotangent.shape[1]
    return pl.pallas_call(
        pack_kernel,
        out_shape=[
            jax.ShapeDtypeStruct((tokens, columns + shared), activations.dtype),
            jax.ShapeDtypeStruct((tokens, columns + width - shared), activations.dtype),
        ],
        in_specs=[anywhere, anywhere],
        out_specs=[whole, whole],
        scratch_shapes=[pltpu.SemaphoreType.DMA((8,))],
        compiler_params=pltpu.CompilerParams(vmem_limit_bytes=60 * 1024 * 1024),
    )(activations, cotangent)


def part(source, total, side, kept, sent):
    for g in range(source.shape[0] // group):
        total[g % 2, g // 2 * group:(g // 2 + 1) * group, :] = source[g * group:(g + 1) * group, :]
    kept[...] = total[side]
    code(total.at[1 - side], sent)


def sums_kernel(place, own, own_up, own_down, cotangent, below, above, far_sent, far_kept, near_sent, near_kept,
                far, near, far_parted, near_parted):
    width = own.shape[1]
    mine, under, over = cotangent[...], below[:, 2 * width + shared:], above[:, 3 * width - shared:]
    far[:width] = product(own_up[...], mine) + product(above[:, width:2 * width], over)
    far[:shared] += product(below[:, 2 * width:2 * width + shared], under)
    far[width:] = product(own_down[...], mine) + product(below[:, width:2 * width], under)
    far[width + shared:] += product(above[:, 2 * width:3 * width - shared], over)
    part(far, far_parted, place[1], far_kept, far_sent)
    near[...] = product(own[...], mine) + product(below[:, :width], under) + product(above[:, :width], over)
    part(near, near_parted, place[1], near_kept, near_sent)


def sums(place, activations, cotangent, from_below, from_above):
    width = activations.shape[1] // ring
    half = width // 2
    columns = cotangent.shape[1]
    outs = [
        jax.ShapeDtypeStruct((width + tail, columns), jnp.int16),
        jax.ShapeDtypeStruct((width, columns), jnp.float32),
        jax.ShapeDtypeStruct((half + tail, columns), jnp.int16),
        jax.ShapeDtypeStruct((half, columns), jnp.float32),
    ]
    inputs = [(activations, 0), (activations, 3), (activations, -3), cotangent, from_below, from_above]
    scratch = [(2 * width, columns), (width, columns), (2, width, columns), (2, half, columns)]
    return on_chunks(sums_kernel, place, inputs, outs, scratch)


def call(kernel, outs, place, *args, scratch=(), micros=1):
    return pl.pallas_call(
        kernel,
        out_shape=[jax.ShapeDtypeStruct(s, d) for s, d in outs],
        in_specs=[pl.BlockSpec(memory_space=pltpu.SMEM)] + [whole] * len(args),
        out_specs=[whole] * len(outs),
        scratch_shapes=[pltpu.VMEM(s, jnp.float32) for s in scratch],
        compiler_params=limit,
        cost_estimate=work(micros),
    )(place, *args)


def rest_kernel(place, kept, message, up, down, sums):
    scale = scales(message)
    for g in range(kept.shape[0] // group):
        sums[g * group:(g + 1) * group, :] = kept[g * group:(g + 1) * group, :] + decoded(message, scale, g)
    rows = kept.shape[0] // 2
    code(sums.at[:rows], up)
    code(sums.at[rows:], down)


def rest(place, kept, message):
    rows, columns = kept.shape
    coded = ((rows // 2 + tail, columns), jnp.int16)
    return call(rest_kernel, [coded, coded], place, kept, message, scratch=[(rows, columns)], micros=5)


def fold_kernel(bit, place, kept, *refs):
    messages, (sent, out, total) = refs[:-3], refs[-3:]
    factors = [scales(m) for m in messages]
    for g in range(kept.shape[0] // group):
        value = kept[g * group:(g + 1) * group, :]
        for m, factor in zip(messages, factors):
            value = value + decoded(m, factor, g)
        total[g % 2, g // 2 * group:(g // 2 + 1) * group, :] = value
    side = place[bit]
    out[...] = total[side]
    code(total.at[1 - side], sent)


def fold(place, bit, kept, messages, micros=1):
    half, columns = kept.shape[0] // 2, kept.shape[1]
    outs = [((half + tail, columns), jnp.int16), ((half, columns), jnp.float32)]
    return call(functools.partial(fold_kernel, bit), outs, place, kept, *messages, scratch=[(2, half, columns)], micros=micros)


def last_kernel(scale, place, kept, message, out):
    out[...] = (kept[...] + decoded(message, scales(message), 0)) * scale


def last(scale, place, kept, message):
    return call(functools.partial(last_kernel, scale), [(kept.shape, jnp.float32)], place, kept, message)[0]


def along_ring(shift):
    return [(y * line + z, ((y + shift) % ring) * line + z) for y in range(ring) for z in range(line)]


def along_line(bit):
    return [(y * line + z, y * line + (z ^ bit)) for y in range(ring) for z in range(line)]


def after(value, *others):
    return lax.optimization_barrier((value, *others))[0]


def outer_sums(local, anchor, layer_fragment):
    chosen = layer_fragment == 0
    order = jnp.cumsum(chosen.astype(jnp.int32))
    picks = [(chosen & (order == i + 1))[:, None] for i in range(2)]
    delta = anchor - local
    total = jnp.stack([jnp.sum(jnp.where(p, delta, 0.0), axis=0) for p in picks])
    groups = lax.axis_size("rep")

    def add_over(total, bit):
        with jax.named_scope("differences_over_replicas"):
            return total + lax.ppermute(total, "rep", [(r, r ^ bit) for r in range(groups)])

    return picks, total, add_over


def outer_step(picks, total, anchor, momentum):
    average = total / lax.axis_size("rep")
    average = jnp.where(picks[0], average[0:1], average[1:2])
    moved = momentum_keep * momentum + average
    mask = picks[0] | picks[1]
    new_anchor = jnp.where(mask, anchor - outer_rate * (average + momentum_keep * moved), anchor)
    return new_anchor, jnp.where(mask, moved, momentum)


def step(inputs, cotangent, local, anchor, momentum, layer_fragment):
    tokens, features = inputs.shape
    at = lax.axis_index("fsdp")
    y, z = lax.div(at, line), lax.rem(at, line)
    place = jnp.stack([y, lax.rem(z, 2), lax.rem(lax.div(z, 2), 2), lax.div(z, 4)]).astype(jnp.int32)

    def ring_move(a, shift):
        return lax.ppermute(a, "fsdp", along_ring(shift))

    def line_move(a, bit):
        return lax.ppermute(a, "fsdp", along_line(bit))

    with jax.named_scope("inputs_to_neighbours"):
        above, below = pack(inputs, cotangent)
        received = [ring_move(above, 1), ring_move(below, -1)]
    picks, total, add_over = outer_sums(local, anchor, layer_fragment)
    total = add_over(add_over(after(total, above), 8), 2)
    sent, kept, near, here = sums(after(place, total), inputs, cotangent, *received)
    with jax.named_scope("along_line_first"):
        arrived = line_move(sent, 1)
        messages = [line_move(near, 1)]
    total = add_over(add_over(after(total, sent), 1), 4)
    up, down = rest(after(place, total), kept, arrived)
    with jax.named_scope("far_along_ring"):
        messages += [ring_move(up, 3), ring_move(down, -3)]
    with jax.named_scope("along_line"):
        sent, here = fold(place, 2, here, messages)
        sent = line_move(sent, 2)
        sent, here = fold(place, 3, here, [sent])
        sent = line_move(sent, 4)
    grad = last(float(tokens * ring * line) ** (-0.5), place, here, sent)
    return (grad, *outer_step(picks, total, anchor, momentum))


def body(activations, key_cotangent, local_params, anchor, momentum, layer_fragment):
    grad, new_anchor, new_momentum = step(
        activations[0], key_cotangent[0], local_params[0], anchor, momentum, layer_fragment
    )
    return (grad[None], new_anchor, new_momentum)


def solution(mesh):
    placed = (
        P("rep", "fsdp", None),
        P("rep", "fsdp", None),
        P("rep", None, "fsdp"),
        P(None, "fsdp"),
        P(None, "fsdp"),
        P(),
    )
    return jax.shard_map(
        body,
        mesh=mesh,
        in_specs=placed,
        out_specs=(P("rep", "fsdp", None), P(None, "fsdp"), P(None, "fsdp")),
        check_vma=False,
    )
```

```python
import functools
import math

import jax
import jax.numpy as jnp
from jax import lax
from jax.experimental import pallas as pl
from jax.experimental.pallas import tpu as pltpu
from jax.sharding import PartitionSpec as P

outer_rate = 0.7
momentum_keep = 0.9
ring, line = 8, 8
group = 64
shared = 128
tail = 16
steps_per_octave = 8.0
top = 32760.0
whole = pl.BlockSpec(memory_space=pltpu.VMEM)
anywhere = pl.BlockSpec(memory_space=pl.ANY)
limit = pltpu.CompilerParams(vmem_limit_bytes=40 * 1024 * 1024)


def work(micros):
    return pl.CostEstimate(flops=0, bytes_accessed=micros * 3000000, transcendentals=0)


def code(values, out):
    count = values.shape[0] // group
    exponents = []
    for g in range(count):
        part = values[g * group:(g + 1) * group, :]
        most = jnp.max(jnp.abs(part), axis=0, keepdims=True)
        exponent = jnp.ceil(jnp.log(jnp.maximum(most, 1e-30)) * (steps_per_octave / math.log(2.0))) + 1.0
        inverse = jnp.exp(exponent * (-math.log(2.0) / steps_per_octave)) * top
        magic = 12582912.0
        coded = (part * inverse + magic) - magic
        out[g * group:(g + 1) * group, :] = coded.astype(jnp.int32).astype(jnp.int16)
        exponents.append(exponent)
    exponents.append(jnp.zeros((tail - count, values.shape[1]), jnp.float32))
    out[count * group:count * group + tail, :] = jnp.concatenate(exponents, axis=0).astype(jnp.int32).astype(jnp.int16)


def scales(message):
    rows = message.shape[0] - tail
    exponents = message[rows:rows + tail, :].astype(jnp.int32).astype(jnp.float32)
    return jnp.exp(exponents * (math.log(2.0) / steps_per_octave)) * (1.0 / top)


def decoded(message, scale, g):
    return message[g * group:(g + 1) * group, :].astype(jnp.int32).astype(jnp.float32) * scale[g:g + 1]


def product(left, right):
    return lax.dot_general(left, right, (((0,), (0,)), ((), ())), preferred_element_type=jnp.float32)


def chunk_of(activations, shift):
    width = activations.shape[1] // ring
    return pl.BlockSpec((activations.shape[0], width), lambda i, place: (0, lax.rem(place[0] + shift + ring, ring)))


def on_chunks(kernel, place, inputs, outs, scratch=(), mebibytes=40):
    full = lambda a: pl.BlockSpec(a.shape, lambda i, place: (0, 0))
    specs = [chunk_of(*a) if isinstance(a, tuple) else full(a) for a in inputs]
    return pl.pallas_call(
        kernel,
        out_shape=outs,
        grid_spec=pltpu.PrefetchScalarGridSpec(
            num_scalar_prefetch=1,
            grid=(1,),
            in_specs=specs,
            out_specs=[full(o) for o in outs],
            scratch_shapes=[pltpu.VMEM(shape, jnp.float32) for shape in scratch],
        ),
        compiler_params=pltpu.CompilerParams(vmem_limit_bytes=mebibytes * 1024 * 1024),
        cost_estimate=work(1),
    )(place, *[a[0] if isinstance(a, tuple) else a for a in inputs])


def pack_kernel(activations, cotangent, above, below, sems):
    width = activations.shape[1] // ring
    y = lax.div(lax.axis_index("fsdp"), line)

    def chunk(shift, start=0, size=width):
        at = lax.rem(y + shift + ring, ring) * width + start
        return activations.at[:, pl.ds(pl.multiple_of(at, 128), size)]

    rest = width - shared
    pieces = [
        (chunk(-1), below, 0),
        (chunk(1), above, 0),
        (chunk(2), below, width),
        (chunk(-2), above, width),
        (chunk(4, shared, rest), below, 2 * width),
        (chunk(4, 0, shared), above, 2 * width),
        (cotangent, below, 2 * width + rest),
        (cotangent, above, 2 * width + shared),
    ]
    copies = [
        pltpu.make_async_copy(piece, message.at[:, pl.ds(start, piece.shape[1])], sems.at[i])
        for i, (piece, message, start) in enumerate(pieces)
    ]
    for c in copies:
        c.start()
    for c in copies:
        c.wait()


def pack(activations, cotangent):
    tokens, width = activations.shape[0], activations.shape[1] // ring
    columns = 2 * width + cotangent.shape[1]
    return pl.pallas_call(
        pack_kernel,
        out_shape=[
            jax.ShapeDtypeStruct((tokens, columns + shared), activations.dtype),
            jax.ShapeDtypeStruct((tokens, columns + width - shared), activations.dtype),
        ],
        in_specs=[anywhere, anywhere],
        out_specs=[whole, whole],
        scratch_shapes=[pltpu.SemaphoreType.DMA((8,))],
        compiler_params=pltpu.CompilerParams(vmem_limit_bytes=60 * 1024 * 1024),
    )(activations, cotangent)


def part(source, total, side, kept, sent):
    for g in range(source.shape[0] // group):
        total[g % 2, g // 2 * group:(g // 2 + 1) * group, :] = source[g * group:(g + 1) * group, :]
    kept[...] = total[side]
    code(total.at[1 - side], sent)


def sums_kernel(place, own, own_up, own_down, cotangent, below, above, far_sent, far_kept, near_sent, near_kept,
                far, near, far_parted, near_parted):
    width = own.shape[1]
    mine, under, over = cotangent[...], below[:, 2 * width + shared:], above[:, 3 * width - shared:]
    far[:width] = product(own_up[...], mine) + product(above[:, width:2 * width], over)
    far[:shared] += product(below[:, 2 * width:2 * width + shared], under)
    far[width:] = product(own_down[...], mine) + product(below[:, width:2 * width], under)
    far[width + shared:] += product(above[:, 2 * width:3 * width - shared], over)
    part(far, far_parted, place[1], far_kept, far_sent)
    near[...] = product(own[...], mine) + product(below[:, :width], under) + product(above[:, :width], over)
    part(near, near_parted, place[1], near_kept, near_sent)


def sums(place, activations, cotangent, from_below, from_above):
    width = activations.shape[1] // ring
    half = width // 2
    columns = cotangent.shape[1]
    outs = [
        jax.ShapeDtypeStruct((width + tail, columns), jnp.int16),
        jax.ShapeDtypeStruct((width, columns), jnp.float32),
        jax.ShapeDtypeStruct((half + tail, columns), jnp.int16),
        jax.ShapeDtypeStruct((half, columns), jnp.float32),
    ]
    inputs = [(activations, 0), (activations, 3), (activations, -3), cotangent, from_below, from_above]
    scratch = [(2 * width, columns), (width, columns), (2, width, columns), (2, half, columns)]
    return on_chunks(sums_kernel, place, inputs, outs, scratch)


def call(kernel, outs, place, *args, scratch=(), micros=1):
    return pl.pallas_call(
        kernel,
        out_shape=[jax.ShapeDtypeStruct(s, d) for s, d in outs],
        in_specs=[pl.BlockSpec(memory_space=pltpu.SMEM)] + [whole] * len(args),
        out_specs=[whole] * len(outs),
        scratch_shapes=[pltpu.VMEM(s, jnp.float32) for s in scratch],
        compiler_params=limit,
        cost_estimate=work(micros),
    )(place, *args)


def rest_kernel(place, kept, message, up, down, sums):
    scale = scales(message)
    for g in range(kept.shape[0] // group):
        sums[g * group:(g + 1) * group, :] = kept[g * group:(g + 1) * group, :] + decoded(message, scale, g)
    rows = kept.shape[0] // 2
    code(sums.at[:rows], up)
    code(sums.at[rows:], down)


def rest(place, kept, message):
    rows, columns = kept.shape
    coded = ((rows // 2 + tail, columns), jnp.int16)
    return call(rest_kernel, [coded, coded], place, kept, message, scratch=[(rows, columns)], micros=5)


def fold_kernel(bit, place, kept, *refs):
    messages, (sent, out, total) = refs[:-3], refs[-3:]
    factors = [scales(m) for m in messages]
    for g in range(kept.shape[0] // group):
        value = kept[g * group:(g + 1) * group, :]
        for m, factor in zip(messages, factors):
            value = value + decoded(m, factor, g)
        total[g % 2, g // 2 * group:(g // 2 + 1) * group, :] = value
    side = place[bit]
    out[...] = total[side]
    code(total.at[1 - side], sent)


def fold(place, bit, kept, messages, micros=1):
    half, columns = kept.shape[0] // 2, kept.shape[1]
    outs = [((half + tail, columns), jnp.int16), ((half, columns), jnp.float32)]
    return call(functools.partial(fold_kernel, bit), outs, place, kept, *messages, scratch=[(2, half, columns)], micros=micros)


def last_kernel(scale, place, kept, message, out):
    out[...] = (kept[...] + decoded(message, scales(message), 0)) * scale


def last(scale, place, kept, message):
    return call(functools.partial(last_kernel, scale), [(kept.shape, jnp.float32)], place, kept, message)[0]


def along_ring(shift):
    return [(y * line + z, ((y + shift) % ring) * line + z) for y in range(ring) for z in range(line)]


def along_line(bit):
    return [(y * line + z, y * line + (z ^ bit)) for y in range(ring) for z in range(line)]


def after(value, *others):
    return lax.optimization_barrier((value, *others))[0]


def outer_sums(local, anchor, layer_fragment):
    chosen = layer_fragment == 0
    order = jnp.cumsum(chosen.astype(jnp.int32))
    picks = [(chosen & (order == i + 1))[:, None] for i in range(2)]
    delta = anchor - local
    total = jnp.stack([jnp.sum(jnp.where(p, delta, 0.0), axis=0) for p in picks])
    groups = lax.axis_size("rep")

    def add_over(total, bit):
        with jax.named_scope("differences_over_replicas"):
            return total + lax.ppermute(total, "rep", [(r, r ^ bit) for r in range(groups)])

    return picks, total, add_over


def outer_step(picks, total, anchor, momentum):
    average = total / lax.axis_size("rep")
    average = jnp.where(picks[0], average[0:1], average[1:2])
    moved = momentum_keep * momentum + average
    mask = picks[0] | picks[1]
    new_anchor = jnp.where(mask, anchor - outer_rate * (average + momentum_keep * moved), anchor)
    return new_anchor, jnp.where(mask, moved, momentum)


def step(inputs, cotangent, local, anchor, momentum, layer_fragment):
    tokens, features = inputs.shape
    at = lax.axis_index("fsdp")
    y, z = lax.div(at, line), lax.rem(at, line)
    place = jnp.stack([y, lax.rem(z, 2), lax.rem(lax.div(z, 2), 2), lax.div(z, 4)]).astype(jnp.int32)

    def ring_move(a, shift):
        return lax.ppermute(a, "fsdp", along_ring(shift))

    def line_move(a, bit):
        return lax.ppermute(a, "fsdp", along_line(bit))

    with jax.named_scope("inputs_to_neighbours"):
        above, below = pack(inputs, cotangent)
        received = [ring_move(above, 1), ring_move(below, -1)]
    picks, total, add_over = outer_sums(local, anchor, layer_fragment)
    total = add_over(after(total, above), 2)
    sent, kept, near, here = sums(after(place, total), inputs, cotangent, *received)
    with jax.named_scope("along_line_first"):
        arrived = line_move(sent, 1)
        messages = [line_move(near, 1)]
    total = add_over(add_over(after(total, sent), 1), 4)
    up, down = rest(after(place, total), kept, arrived)
    with jax.named_scope("far_along_ring"):
        messages += [ring_move(up, 3), ring_move(down, -3)]
    total = add_over(after(total, messages[1]), 8)
    with jax.named_scope("along_line"):
        sent, here = fold(place, 2, here, messages)
        sent = line_move(sent, 2)
        sent, here = fold(place, 3, here, [sent])
        sent = line_move(sent, 4)
    grad = last(float(tokens * ring * line) ** (-0.5), place, here, sent)
    return (grad, *outer_step(picks, total, anchor, momentum))


def body(activations, key_cotangent, local_params, anchor, momentum, layer_fragment):
    grad, new_anchor, new_momentum = step(
        activations[0], key_cotangent[0], local_params[0], anchor, momentum, layer_fragment
    )
    return (grad[None], new_anchor, new_momentum)


def solution(mesh):
    placed = (
        P("rep", "fsdp", None),
        P("rep", "fsdp", None),
        P("rep", None, "fsdp"),
        P(None, "fsdp"),
        P(None, "fsdp"),
        P(),
    )
    return jax.shard_map(
        body,
        mesh=mesh,
        in_specs=placed,
        out_specs=(P("rep", "fsdp", None), P(None, "fsdp"), P(None, "fsdp")),
        check_vma=False,
    )
```

```python
import functools
import math

import jax
import jax.numpy as jnp
from jax import lax
from jax.experimental import pallas as pl
from jax.experimental.pallas import tpu as pltpu
from jax.sharding import PartitionSpec as P

outer_rate = 0.7
momentum_keep = 0.9
ring, line = 8, 8
group = 64
shared = 128
tail = 16
steps_per_octave = 8.0
top = 32760.0
whole = pl.BlockSpec(memory_space=pltpu.VMEM)
anywhere = pl.BlockSpec(memory_space=pl.ANY)
limit = pltpu.CompilerParams(vmem_limit_bytes=40 * 1024 * 1024)


def work(micros):
    return pl.CostEstimate(flops=0, bytes_accessed=micros * 3000000, transcendentals=0)


def code(values, out):
    count = values.shape[0] // group
    exponents = []
    for g in range(count):
        part = values[g * group:(g + 1) * group, :]
        most = jnp.max(jnp.abs(part), axis=0, keepdims=True)
        exponent = jnp.ceil(jnp.log(jnp.maximum(most, 1e-30)) * (steps_per_octave / math.log(2.0))) + 1.0
        inverse = jnp.exp(exponent * (-math.log(2.0) / steps_per_octave)) * top
        magic = 12582912.0
        coded = (part * inverse + magic) - magic
        out[g * group:(g + 1) * group, :] = coded.astype(jnp.int32).astype(jnp.int16)
        exponents.append(exponent)
    exponents.append(jnp.zeros((tail - count, values.shape[1]), jnp.float32))
    out[count * group:count * group + tail, :] = jnp.concatenate(exponents, axis=0).astype(jnp.int32).astype(jnp.int16)


def scales(message):
    rows = message.shape[0] - tail
    exponents = message[rows:rows + tail, :].astype(jnp.int32).astype(jnp.float32)
    return jnp.exp(exponents * (math.log(2.0) / steps_per_octave)) * (1.0 / top)


def decoded(message, scale, g):
    return message[g * group:(g + 1) * group, :].astype(jnp.int32).astype(jnp.float32) * scale[g:g + 1]


def product(left, right):
    return lax.dot_general(left, right, (((0,), (0,)), ((), ())), preferred_element_type=jnp.float32)


def chunk_of(activations, shift):
    width = activations.shape[1] // ring
    return pl.BlockSpec((activations.shape[0], width), lambda i, place: (0, lax.rem(place[0] + shift + ring, ring)))


def on_chunks(kernel, place, inputs, outs, scratch=(), mebibytes=40):
    full = lambda a: pl.BlockSpec(a.shape, lambda i, place: (0, 0))
    specs = [chunk_of(*a) if isinstance(a, tuple) else full(a) for a in inputs]
    return pl.pallas_call(
        kernel,
        out_shape=outs,
        grid_spec=pltpu.PrefetchScalarGridSpec(
            num_scalar_prefetch=1,
            grid=(1,),
            in_specs=specs,
            out_specs=[full(o) for o in outs],
            scratch_shapes=[pltpu.VMEM(shape, jnp.float32) for shape in scratch],
        ),
        compiler_params=pltpu.CompilerParams(vmem_limit_bytes=mebibytes * 1024 * 1024),
        cost_estimate=work(1),
    )(place, *[a[0] if isinstance(a, tuple) else a for a in inputs])


def pack_kernel(activations, cotangent, above, below, sems):
    width = activations.shape[1] // ring
    y = lax.div(lax.axis_index("fsdp"), line)

    def chunk(shift, start=0, size=width):
        at = lax.rem(y + shift + ring, ring) * width + start
        return activations.at[:, pl.ds(pl.multiple_of(at, 128), size)]

    rest = width - shared
    pieces = [
        (chunk(-1), below, 0),
        (chunk(1), above, 0),
        (chunk(2), below, width),
        (chunk(-2), above, width),
        (chunk(4, shared, rest), below, 2 * width),
        (chunk(4, 0, shared), above, 2 * width),
        (cotangent, below, 2 * width + rest),
        (cotangent, above, 2 * width + shared),
    ]
    copies = [
        pltpu.make_async_copy(piece, message.at[:, pl.ds(start, piece.shape[1])], sems.at[i])
        for i, (piece, message, start) in enumerate(pieces)
    ]
    for c in copies:
        c.start()
    for c in copies:
        c.wait()


def pack(activations, cotangent):
    tokens, width = activations.shape[0], activations.shape[1] // ring
    columns = 2 * width + cotangent.shape[1]
    return pl.pallas_call(
        pack_kernel,
        out_shape=[
            jax.ShapeDtypeStruct((tokens, columns + shared), activations.dtype),
            jax.ShapeDtypeStruct((tokens, columns + width - shared), activations.dtype),
        ],
        in_specs=[anywhere, anywhere],
        out_specs=[whole, whole],
        scratch_shapes=[pltpu.SemaphoreType.DMA((8,))],
        compiler_params=pltpu.CompilerParams(vmem_limit_bytes=60 * 1024 * 1024),
    )(activations, cotangent)


def part(source, total, side, kept, sent):
    for g in range(source.shape[0] // group):
        total[g % 2, g // 2 * group:(g // 2 + 1) * group, :] = source[g * group:(g + 1) * group, :]
    kept[...] = total[side]
    code(total.at[1 - side], sent)


def sums_kernel(place, own, own_up, own_down, cotangent, below, above, far_sent, far_kept, near_sent, near_kept,
                far, near, far_parted, near_parted):
    width = own.shape[1]
    mine, under, over = cotangent[...], below[:, 2 * width + shared:], above[:, 3 * width - shared:]
    far[:width] = product(own_up[...], mine) + product(above[:, width:2 * width], over)
    far[:shared] += product(below[:, 2 * width:2 * width + shared], under)
    far[width:] = product(own_down[...], mine) + product(below[:, width:2 * width], under)
    far[width + shared:] += product(above[:, 2 * width:3 * width - shared], over)
    part(far, far_parted, place[1], far_kept, far_sent)
    near[...] = product(own[...], mine) + product(below[:, :width], under) + product(above[:, :width], over)
    part(near, near_parted, place[1], near_kept, near_sent)


def sums(place, activations, cotangent, from_below, from_above):
    width = activations.shape[1] // ring
    half = width // 2
    columns = cotangent.shape[1]
    outs = [
        jax.ShapeDtypeStruct((width + tail, columns), jnp.int16),
        jax.ShapeDtypeStruct((width, columns), jnp.float32),
        jax.ShapeDtypeStruct((half + tail, columns), jnp.int16),
        jax.ShapeDtypeStruct((half, columns), jnp.float32),
    ]
    inputs = [(activations, 0), (activations, 3), (activations, -3), cotangent, from_below, from_above]
    scratch = [(2 * width, columns), (width, columns), (2, width, columns), (2, half, columns)]
    return on_chunks(sums_kernel, place, inputs, outs, scratch)


def call(kernel, outs, place, *args, scratch=(), micros=1):
    return pl.pallas_call(
        kernel,
        out_shape=[jax.ShapeDtypeStruct(s, d) for s, d in outs],
        in_specs=[pl.BlockSpec(memory_space=pltpu.SMEM)] + [whole] * len(args),
        out_specs=[whole] * len(outs),
        scratch_shapes=[pltpu.VMEM(s, jnp.float32) for s in scratch],
        compiler_params=limit,
        cost_estimate=work(micros),
    )(place, *args)


def rest_kernel(place, kept, message, up, down, sums):
    scale = scales(message)
    for g in range(kept.shape[0] // group):
        sums[g * group:(g + 1) * group, :] = kept[g * group:(g + 1) * group, :] + decoded(message, scale, g)
    rows = kept.shape[0] // 2
    code(sums.at[:rows], up)
    code(sums.at[rows:], down)


def rest(place, kept, message):
    rows, columns = kept.shape
    coded = ((rows // 2 + tail, columns), jnp.int16)
    return call(rest_kernel, [coded, coded], place, kept, message, scratch=[(rows, columns)], micros=5)


def fold_kernel(bit, place, kept, *refs):
    messages, (sent, out, total) = refs[:-3], refs[-3:]
    factors = [scales(m) for m in messages]
    for g in range(kept.shape[0] // group):
        value = kept[g * group:(g + 1) * group, :]
        for m, factor in zip(messages, factors):
            value = value + decoded(m, factor, g)
        total[g % 2, g // 2 * group:(g // 2 + 1) * group, :] = value
    side = place[bit]
    out[...] = total[side]
    code(total.at[1 - side], sent)


def fold(place, bit, kept, messages, micros=1):
    half, columns = kept.shape[0] // 2, kept.shape[1]
    outs = [((half + tail, columns), jnp.int16), ((half, columns), jnp.float32)]
    return call(functools.partial(fold_kernel, bit), outs, place, kept, *messages, scratch=[(2, half, columns)], micros=micros)


def last_kernel(scale, place, kept, message, out):
    out[...] = (kept[...] + decoded(message, scales(message), 0)) * scale


def last(scale, place, kept, message):
    return call(functools.partial(last_kernel, scale), [(kept.shape, jnp.float32)], place, kept, message)[0]


def along_ring(shift):
    return [(y * line + z, ((y + shift) % ring) * line + z) for y in range(ring) for z in range(line)]


def along_line(bit):
    return [(y * line + z, y * line + (z ^ bit)) for y in range(ring) for z in range(line)]


def after(value, *others):
    return lax.optimization_barrier((value, *others))[0]


def outer_sums(local, anchor, layer_fragment):
    chosen = layer_fragment == 0
    order = jnp.cumsum(chosen.astype(jnp.int32))
    picks = [(chosen & (order == i + 1))[:, None] for i in range(2)]
    delta = anchor - local
    total = jnp.stack([jnp.sum(jnp.where(p, delta, 0.0), axis=0) for p in picks])
    groups = lax.axis_size("rep")

    def add_over(total, bit):
        with jax.named_scope("differences_over_replicas"):
            return total + lax.ppermute(total, "rep", [(r, r ^ bit) for r in range(groups)])

    return picks, total, add_over


def outer_step(picks, total, anchor, momentum):
    average = total / lax.axis_size("rep")
    average = jnp.where(picks[0], average[0:1], average[1:2])
    moved = momentum_keep * momentum + average
    mask = picks[0] | picks[1]
    new_anchor = jnp.where(mask, anchor - outer_rate * (average + momentum_keep * moved), anchor)
    return new_anchor, jnp.where(mask, moved, momentum)


def step(inputs, cotangent, local, anchor, momentum, layer_fragment):
    tokens, features = inputs.shape
    at = lax.axis_index("fsdp")
    y, z = lax.div(at, line), lax.rem(at, line)
    place = jnp.stack([y, lax.rem(z, 2), lax.rem(lax.div(z, 2), 2), lax.div(z, 4)]).astype(jnp.int32)

    def ring_move(a, shift):
        return lax.ppermute(a, "fsdp", along_ring(shift))

    def line_move(a, bit):
        return lax.ppermute(a, "fsdp", along_line(bit))

    with jax.named_scope("inputs_to_neighbours"):
        above, below = pack(inputs, cotangent)
        received = [ring_move(above, 1), ring_move(below, -1)]
    picks, total, add_over = outer_sums(local, anchor, layer_fragment)
    total = add_over(after(total, above), 2)
    sent, kept, near, here = sums(after(place, total), inputs, cotangent, *received)
    with jax.named_scope("along_line_first"):
        arrived = line_move(sent, 1)
    total = add_over(add_over(after(total, sent), 1), 4)
    with jax.named_scope("near_along_line"):
        messages = [line_move(after(near, total), 1)]
    up, down = rest(after(place, total), kept, arrived)
    with jax.named_scope("far_along_ring"):
        messages += [ring_move(up, 3), ring_move(down, -3)]
    total = add_over(after(total, messages[0], messages[1]), 8)
    with jax.named_scope("along_line"):
        sent, here = fold(place, 2, here, messages)
        sent = line_move(sent, 2)
        sent, here = fold(place, 3, here, [sent])
        sent = line_move(sent, 4)
    grad = last(float(tokens * ring * line) ** (-0.5), place, here, sent)
    return (grad, *outer_step(picks, total, anchor, momentum))


def body(activations, key_cotangent, local_params, anchor, momentum, layer_fragment):
    grad, new_anchor, new_momentum = step(
        activations[0], key_cotangent[0], local_params[0], anchor, momentum, layer_fragment
    )
    return (grad[None], new_anchor, new_momentum)


def solution(mesh):
    placed = (
        P("rep", "fsdp", None),
        P("rep", "fsdp", None),
        P("rep", None, "fsdp"),
        P(None, "fsdp"),
        P(None, "fsdp"),
        P(),
    )
    return jax.shard_map(
        body,
        mesh=mesh,
        in_specs=placed,
        out_specs=(P("rep", "fsdp", None), P(None, "fsdp"), P(None, "fsdp")),
        check_vma=False,
    )
```
